32 devices in a mesh: member: 4 (over x, core), col: 8 (over z, y).
Axes of the slice: x: 2, y: 2, z: 4, core: 2. Of those that a mesh axis runs over, the one named last changes fastest.
Arguments:
- increment: bfloat16 [128, 137, 256], P(('member', 'col')), parts along dimension 0, may hold values from -6 to 6
- jacobian: bfloat16 [3072, 128, 137], P(('member', 'col')), parts along dimension 0, may hold values from -0.5 to 0.5
- innovation: bfloat16 [3072, 128, 256], P(('member', 'col')), parts along dimension 0, may hold values from -6 to 6
- inv_variance: float32 [128], replicated, may hold values from 0.25 to 4
- counts: int32 [3072, 256], P(('member', 'col')), parts along dimension 0, may hold values from 0 to 3
- owner: int32 [768, 1], replicated, may hold values from 0 to 7; in each aligned block of 96 rows (0 to 95, 96 to 191, ...) at most 24 rows name the same one
- local_block: int32 [768], replicated, may hold values from 0 to 3
Outputs:
- gradient: float32 [128, 137, 256], P(('member', 'col')), parts along dimension 0
The draws below stay inside these ranges and needn't reach their ends.
There are 4 independent parts, one for each index of `member`. The reference program is written for one: setup_inputs(seed, part) draws one part's arguments, and reference() takes and returns one part's arrays. A program takes and returns all parts, laid end to end along the dimension named above; an argument that names none is the same for every part. Nothing has to cross between parts.
Inputs may be any that keep to these rules, and one draw needn't show every extreme that they name: `owner`: within the rows of one index of col (aligned blocks of 96 rows), no index of col appears more than 24 times, and some block reaches 24.
All inputs are finite; a program needn't handle non-finite values.
Results may differ from the reference program's by a relative error of at most 0.0012.
Values may be sent and summed in bfloat16 or wider, within the bound.
No kernel may reach another device: no remote copies, remote signals or barrier semaphores. Data moves between devices by JAX's collectives and lax.ppermute only.
A program may use at most 128 MiB of HBM per device.

```python
import math
import jax
import jax.numpy as jnp
import numpy as np
from jax import lax

LEV = 137
NCH = 128
COLW = 256
CB_DEV = 4
OB_DEV = 96
NCB = 32
NOB = 768
CAP = 24
N_COL = 8


def touch_ends(array, rng, smallest, largest):
    longest = array.shape.index(max(array.shape))
    spots = []
    for shift in (0, 1):
        where = [jax.random.randint(jax.random.fold_in(rng, axis), (), 0, length) for axis, length in enumerate(array.shape)]
        where[longest] = (where[longest] + shift) % array.shape[longest]
        spots.append(tuple(where))
    return array.at[spots[0]].set(smallest).at[spots[1]].set(largest)


def block_scale(key, dims, split, smallest, top_value):
    def one(position, shards_of):
        steps = jax.random.uniform(jax.random.fold_in(jax.random.fold_in(key, 6), position), (shards_of,), jnp.float32, smallest / len(split), top_value / len(split))
        return jnp.repeat(jnp.exp(steps), dims[position] // shards_of).reshape((-1,) + (1,) * (len(dims) - position - 1))

    factor_of = one(*split[0])
    for cut in split[1:]:
        factor_of = factor_of * one(*cut)
    return factor_of


def assign_block(key, own, number, rows, amount, top, reach, lean):
    ranking = jax.random.permutation(key, amount)
    heavy_load, usual = load_shares(amount, rows * top, reach, lean, True), load_shares(amount, rows * top, reach, lean, False)
    places = jnp.arange(amount)

    def named(lengths, offset_by):
        used = int((lengths > 0).sum())
        fixed = max(1, used // 4)
        passed = fixed + (places - fixed + offset_by * (used - fixed)) % max(1, amount - fixed)
        return jnp.zeros((amount,), jnp.int32).at[ranking[jnp.where(places < fixed, places, passed)]].set(jnp.asarray(lengths, jnp.int32))

    lengths = jnp.where(number % 4 == 0, named(heavy_load, number // 4), named(usual, number - number // 4 - 1))
    mixed = jax.random.permutation(jax.random.fold_in(own, 3), amount)
    donor, receiver = mixed[0:amount // 2 * 2:2], mixed[1:amount // 2 * 2:2]
    room = jnp.minimum(lengths[donor] - 1, reach - lengths[receiver]) // 2
    room = jnp.where((donor == ranking[0]) | (receiver == ranking[0]) | (lengths[receiver] == 0), 0, jnp.maximum(room, 0))
    passed = jax.random.randint(jax.random.fold_in(own, 4), (amount // 2,), 0, 1 << 20) % (room + 1)
    lengths = lengths.at[donor].add(-passed).at[receiver].add(passed)
    members = jnp.searchsorted(jnp.cumsum(lengths), jnp.arange(rows * top), side="right").astype(jnp.int32)
    table = members.reshape(top, rows).T
    table = table[jax.random.permutation(jax.random.fold_in(own, 1), rows)]
    offset_by = jax.random.randint(jax.random.fold_in(own, 2), (rows, 1), 0, top)
    return jnp.take_along_axis(table, (jnp.arange(top)[None, :] + offset_by) % top, axis=1)


def load_shares(count, total, most, lean, full):
    weights = [(1 << 20) // math.isqrt(standing ** lean) + 1 for standing in range(1, count + 1)]
    largest = most if full else min(most, max(-(-total // count), total * weights[0] // sum(weights)))
    least = 1 if total - largest >= count - 1 else 0
    given, spare = [largest] + [least] * (count - 1), total - largest - least * (count - 1)
    while spare > 0:
        movable = [i for i in range(1, count) if given[i] < largest] or [i for i in range(1, count) if given[i] < most]
        whole, remaining = sum([weights[i] for i in movable]), spare
        for i in movable:
            more = min(most - given[i], max(1, remaining * weights[i] // whole), spare)
            given[i] = given[i] + more
            spare = spare - more
    return np.array(given)


def gaussian(own_key, dims, deviation, limit, shards=(), dtype=jnp.bfloat16):
    array = jax.random.normal(own_key, dims, jnp.float32) * deviation
    if len(shards) > 0:
        array = block_scale(own_key, dims, shards, -0.22, 0.18) * array
    return jnp.clip(array, min=-limit, max=limit).astype(dtype)


def setup_inputs(seed: int = 0, part: int = 0) -> dict:
    splits = jax.random.split(jax.random.key(seed), 8)
    part_splits = jax.random.split(jax.random.fold_in(splits[7], part), 8)
    increment = gaussian(part_splits[0], (NCB, LEV, COLW), 1.0, 6.0, ((0, 8),))
    jacobian = gaussian(part_splits[1], (NOB, NCH, LEV), LEV ** -0.5, 0.5, ((0, 8),))
    innovation = gaussian(part_splits[2], (NOB, NCH, COLW), 1.0, 6.0, ((0, 8),))
    inv_variance = jnp.clip(jnp.exp(jax.random.uniform(splits[3], (NCH,), jnp.float32, math.log(0.25), math.log(4.0))), 0.25, 4.0)
    counts = touch_ends(jax.random.randint(part_splits[4], (NOB, COLW), 0, 4), jax.random.fold_in(part_splits[4], 1), 0, 3).astype(jnp.int32)
    owner_keys = jax.random.split(jax.random.fold_in(splits[5], 1), NOB // OB_DEV)
    owner_turns = jax.random.permutation(jax.random.fold_in(splits[5], 3), NOB // OB_DEV)
    owner = jax.vmap(lambda own, number: assign_block(jax.random.fold_in(splits[5], 2), own, number, OB_DEV, N_COL, 1, CAP, 2))(owner_keys, owner_turns).reshape((NOB, 1))
    local_block = touch_ends(jax.random.randint(splits[6], (NOB,), 0, CB_DEV), jax.random.fold_in(splits[6], 1), 0, CB_DEV - 1).astype(jnp.int32)
    return {"increment": increment, "jacobian": jacobian, "innovation": innovation, "inv_variance": inv_variance, "counts": counts, "owner": owner, "local_block": local_block}


def reference(increment, jacobian, innovation, inv_variance, counts, owner, local_block):
    col_block = (owner[:, 0] * CB_DEV + local_block).astype(jnp.int32)
    groups = NOB // OB_DEV
    jac_groups = jacobian.reshape(groups, OB_DEV, NCH, LEV)
    inn_groups = innovation.reshape(groups, OB_DEV, NCH, COLW)
    cnt_groups = counts.reshape(groups, OB_DEV, COLW)
    blk_groups = col_block.reshape(groups, OB_DEV)

    def step(total, item):
        jac_part, inn_part, cnt_part, blk_part = item
        profile = increment[blk_part]
        jac_float = jac_part.astype(jnp.float32)
        evolved = jnp.einsum('bcl,blw->bcw', jac_float, profile.astype(jnp.float32))
        resid = evolved - inn_part.astype(jnp.float32)
        weighted = (inv_variance[None, :, None] * cnt_part[:, None, :].astype(jnp.float32) * resid).astype(jnp.bfloat16)
        adjoint = jnp.einsum('bcl,bcw->blw', jac_float, weighted.astype(jnp.float32))
        total = total + jax.ops.segment_sum(adjoint, blk_part, num_segments=NCB)
        return total, None

    start = jnp.zeros((NCB, LEV, COLW), jnp.float32)
    gradient, unused = lax.scan(step, start, (jac_groups, inn_groups, cnt_groups, blk_groups))
    return gradient
```

```python
import functools

import jax
import jax.numpy as jnp
from jax import lax
from jax.experimental import pallas as pl
from jax.experimental.pallas import tpu as pltpu
from jax.sharding import PartitionSpec as P

TOP = 32000.0
LANES = 16
UNROLL = 4


def pack(x, rows):
    largest = jnp.maximum(jnp.max(jnp.abs(x), axis=0, keepdims=True), 1e-30)
    power = jnp.ceil(jnp.log2(largest))
    part = jnp.ceil(largest * jnp.exp2(14.0 - power))
    value = jnp.round(x * (TOP / (part * jnp.exp2(power - 14.0))))
    row = lax.broadcasted_iota(jnp.int32, x.shape, 0)
    value = jnp.where(row == rows, power, jnp.where(row == rows + 1, part, value))
    return value.astype(jnp.int32).astype(jnp.int16)


def unpack(coded, rows):
    value = coded.astype(jnp.int32).astype(jnp.float32)
    scale = value[rows + 1 : rows + 2] * jnp.exp2(value[rows : rows + 1] - 14.0) * (1.0 / TOP)
    row = lax.broadcasted_iota(jnp.int32, value.shape, 0)
    return jnp.where(row < rows, value * scale, 0.0)


def term_kernel(rows, n, inner, back, other, has_init, packed, table, inc, jac, inn, cnt, iv, *refs):
    out, acc = refs[-2:]
    blocks = inc.shape[0]
    outer = n // inner
    me = table[0]
    line, place = me // inner, lax.rem(me, inner)
    line = lax.rem(line + outer - back, outer)
    place = lax.rem(place + other, inner)
    holder = line * inner + place
    first, last = table[1 + holder], table[2 + holder]
    for l in range(blocks):
        acc[l] = unpack(refs[0][l], rows) if has_init else jnp.zeros(acc.shape[1:], jnp.float32)
    variance = iv[...]

    def step(i, carry):
        terms = []
        for u in range(UNROLL):
            p = first + i * UNROLL + u
            entry = table[2 + n + jnp.minimum(p, last - 1)]
            b, l = entry // blocks, lax.rem(entry, blocks)
            live = (p < last).astype(jnp.float32)
            evolved = lax.dot_general(
                jac[b], inc[l], (((0,), (0,)), ((), ())), preferred_element_type=jnp.float32
            )
            weight = variance * (cnt[pl.ds(b, 1), :].astype(jnp.float32) * live)
            weighted = (weight * (evolved - inn[b].astype(jnp.float32))).astype(jnp.bfloat16)
            terms.append((l, jnp.dot(jac[b], weighted, preferred_element_type=jnp.float32)))
        for l, t in terms:
            acc[l] += t
        return carry

    lax.fori_loop(0, (last - first + UNROLL - 1) // UNROLL, step, 0)
    for l in range(blocks):
        out[l] = pack(acc[l], rows) if packed else acc[l]


def term(rows, n, inner, back, other, packed, local, inc, init=None):
    table, jac, inn, cnt, iv = local
    smem = pl.BlockSpec(memory_space=pltpu.SMEM)
    vmem = pl.BlockSpec(memory_space=pltpu.VMEM)
    operands = [table, inc, jac, inn, cnt, iv] + ([] if init is None else [init])
    flops = 4 * (jac.shape[0] // n) * jac.shape[1] * jac.shape[2] * inc.shape[2]
    return pl.pallas_call(
        functools.partial(term_kernel, rows, n, inner, back, other, init is not None, packed),
        out_shape=jax.ShapeDtypeStruct(inc.shape, jnp.int16 if packed else jnp.float32),
        in_specs=[smem] + [vmem] * (len(operands) - 1),
        out_specs=vmem,
        scratch_shapes=[pltpu.VMEM(inc.shape, jnp.float32)],
        compiler_params=pltpu.CompilerParams(vmem_limit_bytes=24 * 2**20),
        cost_estimate=pl.CostEstimate(flops=flops, bytes_accessed=8 * 2**20, transcendentals=0),
    )(*operands)


def total_kernel(rows, own, *refs):
    out = refs[-1]
    for l in range(own.shape[0]):
        total = own[l]
        for coded in refs[:-1]:
            total = total + unpack(coded[l], rows)
        out[l] = total[:rows]


def total(rows, own, coded):
    vmem = pl.BlockSpec(memory_space=pltpu.VMEM)
    shape = (own.shape[0], rows, own.shape[2])
    return pl.pallas_call(
        functools.partial(total_kernel, rows),
        out_shape=jax.ShapeDtypeStruct(shape, jnp.float32),
        in_specs=[vmem] * (1 + len(coded)),
        out_specs=vmem,
        compiler_params=pltpu.CompilerParams(vmem_limit_bytes=24 * 2**20),
        cost_estimate=pl.CostEstimate(flops=2**20, bytes_accessed=2**22, transcendentals=0),
    )(own, *coded)


def sorted_table(owner, local_block, me, n, obs, blocks):
    rows = lax.dynamic_slice_in_dim(owner[:, 0], me * obs, obs)
    local = lax.dynamic_slice_in_dim(local_block, me * obs, obs)
    index = jnp.arange(obs, dtype=jnp.int32)
    key = (rows * blocks + local) * obs + index
    place = jnp.sum(key[None, :] < key[:, None], axis=1, dtype=jnp.int32)
    entry = index * blocks + local
    order = jnp.sum(jnp.where(place[None, :] == index[:, None], entry[None, :], 0), axis=1, dtype=jnp.int32)
    first = jnp.sum(rows[None, :] < jnp.arange(n + 1, dtype=jnp.int32)[:, None], axis=1, dtype=jnp.int32)
    return jnp.concatenate([me.astype(jnp.int32)[None], first, order])


def body(n, increment, jacobian, innovation, inv_variance, counts, owner, local_block):
    obs, channels, rows = jacobian.shape
    blocks = increment.shape[0]
    inner = 2 if n % 2 == 0 else 1
    outer = n // inner
    spare = -(rows + 2) % LANES + 2
    me = lax.axis_index("col")

    def along(x, shift):
        return lax.ppermute(
            x, "col", [(i, (i // inner + shift) % outer * inner + i % inner) for i in range(n)]
        )

    def across(x):
        return lax.ppermute(x, "col", [(i, i // inner * inner + (i + 1) % inner) for i in range(n)])

    inc = jnp.pad(increment, ((0, 0), (0, spare), (0, 0)))
    jac = jnp.pad(jnp.transpose(jacobian, (0, 2, 1)), ((0, 0), (0, spare), (0, 0)))
    table = sorted_table(owner, local_block, me, n, obs, blocks)
    local = (table, jac, innovation, counts, inv_variance[:, None])

    near = [inc]
    for back in range(1, outer):
        near.append(along(near[-1], 1))
    far = [across(x) for x in near] if inner > 1 else [None] * outer
    own = term(rows, n, inner, 0, 0, False, local, inc)
    arrived = []
    for back in range(outer):
        passed = None
        if inner > 1:
            passed = across(term(rows, n, inner, back, 1, True, local, far[back]))
        if back == 0:
            arrived += [] if passed is None else [passed]
        else:
            arrived.append(along(term(rows, n, inner, back, 0, True, local, near[back], passed), -back))
    return total(rows, own, arrived)


def solution(mesh):
    in_specs = (
        P(("member", "col"), None, None),
        P(("member", "col"), None, None),
        P(("member", "col"), None, None),
        P(),
        P(("member", "col"), None),
        P(),
        P(),
    )
    out_specs = P(("member", "col"), None, None)
    run = functools.partial(body, mesh.shape["col"])
    return jax.shard_map(run, mesh=mesh, in_specs=in_specs, out_specs=out_specs, check_vma=False)
```

```python
import functools

import jax
import jax.numpy as jnp
import numpy as np
from jax import lax
from jax.experimental import pallas as pl
from jax.experimental.pallas import tpu as pltpu
from jax.sharding import PartitionSpec as P

TOP = 32000.0
LANES = 16
UNROLL = 6


def pack(x, rows):
    largest = jnp.maximum(jnp.max(jnp.abs(x), axis=0, keepdims=True), 1e-30)
    power = jnp.ceil(jnp.log2(largest))
    part = jnp.ceil(largest * jnp.exp2(14.0 - power))
    value = jnp.round(x * (TOP / (part * jnp.exp2(power - 14.0))))
    row = lax.broadcasted_iota(jnp.int32, x.shape, 0)
    value = jnp.where(row == rows, power, jnp.where(row == rows + 1, part, value))
    return value.astype(jnp.int32).astype(jnp.int16)


def unpack(coded, rows):
    value = coded.astype(jnp.int32).astype(jnp.float32)
    scale = value[rows + 1 : rows + 2] * jnp.exp2(value[rows : rows + 1] - 14.0) * (1.0 / TOP)
    return value * scale


def term_kernel(n, which, count, packed, table, inc, jac, inn, cnt, iv, *refs):
    out, acc = refs[-2:]
    blocks, rows = inc.shape[:2]
    first, last = table[which], table[n + which]
    for l in range(blocks):
        acc[l] = jnp.zeros(acc.shape[1:], jnp.float32)
        if count:
            acc[l, :rows] = sum(unpack(coded[l], rows)[:rows] for coded in refs[:count])
    variance = iv[:, :1]

    def step(i, carry):
        terms = []
        for u in range(UNROLL):
            p = first + i * UNROLL + u
            entry = table[2 * n + jnp.minimum(p, last - 1)]
            b, l = entry // blocks, lax.rem(entry, blocks)
            live = (p < last).astype(jnp.float32)
            evolved = lax.dot_general(
                jac[b], inc[l], (((0,), (0,)), ((), ())), preferred_element_type=jnp.float32
            )
            weight = variance * (cnt[pl.ds(b, 1), :].astype(jnp.float32) * live)
            weighted = (weight * (evolved - inn[b].astype(jnp.float32))).astype(jnp.bfloat16)
            terms.append((l, jnp.dot(jac[b], weighted, preferred_element_type=jnp.float32)))
        for l, t in terms:
            acc[l, :rows] += t
        return carry

    lax.fori_loop(0, (last - first + UNROLL - 1) // UNROLL, step, 0)
    for l in range(blocks):
        out[l] = pack(acc[l], rows) if packed else acc[l, :rows]


def term(padded, n, which, packed, local, inc, *coded):
    table, jac, inn, cnt, iv = local
    smem = pl.BlockSpec(memory_space=pltpu.SMEM)
    vmem = pl.BlockSpec(memory_space=pltpu.VMEM)
    operands = [table, inc, jac, inn, cnt, iv, *coded]

    def shape(dtype, rows):
        return jax.ShapeDtypeStruct((inc.shape[0], rows, inc.shape[2]), dtype)

    return pl.pallas_call(
        functools.partial(term_kernel, n, which, len(coded), packed),
        out_shape=shape(jnp.int16, padded) if packed else shape(jnp.float32, inc.shape[1]),
        in_specs=[smem] + [vmem] * (len(operands) - 1),
        out_specs=vmem,
        scratch_shapes=[pltpu.VMEM((inc.shape[0], padded, inc.shape[2]), jnp.float32)],
        compiler_params=pltpu.CompilerParams(vmem_limit_bytes=16 * 2**20),
        cost_estimate=pl.CostEstimate(flops=2**20, bytes_accessed=8 * 2**20, transcendentals=0),
    )(*operands)


def order(outer):
    end = outer - 1
    if outer < 4:
        todo = [(kind, k) for k in range(1, outer) for kind in "zAy"]
        todo += [(kind, 0) for kind in "OBPs"]
        todo += [(kind, k) for k in range(1, outer) for kind in "BPs"]
        return todo + [(kind, k) for k in range(1, outer) for kind in "STr"]
    todo = [("z", end), ("A", 1), ("O", 0), ("z", 2), ("y", 1), ("B", 0), ("w", end), ("P", 0)]
    for k in range(2, end):
        todo += [("A", k), ("z", k + 1), ("y", k)] if k + 1 < end else [("A", k), ("y", k)]
        todo += [(kind, k - 1) for kind in "BPs"]
        if k > 3:
            todo += [(kind, k - 3) for kind in "STr"]
    todo += [(kind, end - 1) for kind in "BPs"]
    todo += [(kind, end) for kind in "ABPs"]
    todo += [(kind, k) for k in range(max(end - 3, 1), end) for kind in "STr"]
    return todo + [("s", 0), ("S", end), ("T", end), ("r", end)]


def at_hand_kernel(jac, inn, iv, turned, copied, column, whole, jac_sem, inn_sem):
    count = jac_sem.shape[0]
    some = jac.shape[1] // count
    copy = pltpu.make_async_copy(inn, copied, inn_sem)
    parts = [
        pltpu.make_async_copy(jac.at[:, pl.ds(i * some, some)], whole.at[:, pl.ds(i * some, some)], jac_sem.at[i])
        for i in range(count)
    ]
    for part in parts:
        part.start()
    copy.start()
    column[...] = jnp.swapaxes(jnp.broadcast_to(iv[...], column.shape[::-1]), 0, 1)
    for i, part in enumerate(parts):
        part.wait()
        turned[pl.ds(i * some, some)] = jnp.swapaxes(whole[:, pl.ds(i * some, some)], 0, 1)
    copy.wait()


def at_hand(jacobian, innovation, inv_variance):
    obs, channels, levels = jacobian.shape
    some = LANES if obs % LANES == 0 else obs
    hbm, vmem = pl.BlockSpec(memory_space=pltpu.HBM), pl.BlockSpec(memory_space=pltpu.VMEM)
    return pl.pallas_call(
        at_hand_kernel,
        out_shape=(
            pltpu.VMEM((obs, levels, channels), jacobian.dtype),
            pltpu.VMEM(innovation.shape, innovation.dtype),
            pltpu.VMEM((channels, 8), inv_variance.dtype),
        ),
        in_specs=[hbm, hbm, vmem],
        out_specs=(vmem, vmem, vmem),
        scratch_shapes=[
            pltpu.VMEM((levels, obs, channels), jacobian.dtype),
            pltpu.SemaphoreType.DMA((obs // some,)),
            pltpu.SemaphoreType.DMA(()),
        ],
        compiler_params=pltpu.CompilerParams(vmem_limit_bytes=24 * 2**20),
        cost_estimate=pl.CostEstimate(flops=2**20, bytes_accessed=10 * 2**20, transcendentals=0),
    )(
        pltpu.with_memory_space_constraint(jnp.transpose(jacobian, (2, 0, 1)), pltpu.HBM),
        pltpu.with_memory_space_constraint(innovation, pltpu.HBM),
        inv_variance[None, :],
    )


def total_kernel(own, *refs):
    out = refs[-1]
    rows = own.shape[1]
    for l in range(own.shape[0]):
        total = own[l]
        for coded in refs[:-1]:
            total = total + unpack(coded[l], rows)[:rows]
        out[:, l, :] = total


def total(own, coded):
    vmem = pl.BlockSpec(memory_space=pltpu.VMEM)
    blocks, rows, columns = own.shape
    levels_first = pl.pallas_call(
        total_kernel,
        out_shape=jax.ShapeDtypeStruct((rows, blocks, columns), own.dtype),
        in_specs=[vmem] * (1 + len(coded)),
        out_specs=vmem,
        compiler_params=pltpu.CompilerParams(vmem_limit_bytes=16 * 2**20),
        cost_estimate=pl.CostEstimate(flops=2**20, bytes_accessed=8 * 2**20, transcendentals=0),
    )(own, *coded)
    return jnp.transpose(levels_first, (1, 0, 2))


def folded(count):
    return list(range(0, 1)) + list(range(1, count, 2)) + list(range((count - 1) // 2 * 2, 0, -2))


def after(x, gate):
    return lax.optimization_barrier((x, gate))[0]


def sorted_table(owner, local_block, me, holders, obs, blocks):
    rows = lax.dynamic_slice_in_dim(owner[:, 0], me * obs, obs)
    local = lax.dynamic_slice_in_dim(local_block, me * obs, obs)
    index = jnp.arange(obs, dtype=jnp.int32)
    key = (rows * blocks + local) * obs + index
    place = jnp.sum(key[None, :] < key[:, None], axis=1, dtype=jnp.int32)
    entry = index * blocks + local
    order = jnp.sum(jnp.where(place[None, :] == index[:, None], entry[None, :], 0), axis=1, dtype=jnp.int32)
    first = jnp.sum(rows[None, :] < holders[:, None], axis=1, dtype=jnp.int32)
    last = jnp.sum(rows[None, :] <= holders[:, None], axis=1, dtype=jnp.int32)
    return jnp.concatenate([first, last, order])


def body(n, increment, jacobian, innovation, inv_variance, counts, owner, local_block):
    obs, channels, rows = jacobian.shape
    blocks = increment.shape[0]
    inner = 2
    outer = n // inner
    padded = -(-(rows + 2) // LANES) * LANES
    me = lax.axis_index("col")

    ring = folded(outer)

    def along(x, shift):
        lines = [(ring[p], ring[(p + shift) % outer]) for p in range(outer)]
        return lax.ppermute(x, "col", [(a * inner + r, b * inner + r) for a, b in lines for r in range(inner)])

    def across(x):
        return lax.ppermute(x, "col", [(i, i // inner * inner + (i + 1) % inner) for i in range(n)])

    inc = increment
    seat = {line: p for p, line in enumerate(ring)}
    holders = np.array(
        [
            [ring[(seat[i // inner] - back) % outer] * inner + (i + other) % inner for back in range(outer) for other in range(inner)]
            for i in range(n)
        ],
        np.int32,
    )
    table = sorted_table(owner, local_block, me, jnp.asarray(holders)[me], obs, blocks)
    jac, inn, variance = at_hand(jacobian, innovation, inv_variance)
    local = (table, jac, inn, counts, variance)

    coming = {"B0": across(inc)}
    if outer > 1:
        coming["A1"] = along(inc, 1)
    seen, made, gate = {"A0": inc}, {}, ()
    for kind, back in order(outer):
        name = f"{kind}{back}"
        if kind in "ABS":
            seen[name] = gate = after(coming[name], gate)
        elif kind == "z":
            source, shift = (seen[f"A{back - 1}"], 1) if back < outer - 1 else (inc, -1)
            coming[f"A{back}"] = along(after(source, gate), shift)
        elif kind == "y":
            coming[f"B{back}"] = across(after(seen[f"A{back}"], gate))
        elif kind == "w":
            coming[f"B{back}"] = along(after(seen["B0"], gate), -1)
        elif kind == "O":
            own = gate = term(padded, n, 0, False, local, inc)
        elif kind == "P":
            made[name] = gate = term(padded, n, back * inner + 1, True, local, after(seen[f"B{back}"], gate))
        elif kind == "s":
            coming[f"S{back}"] = across(after(made[f"P{back}"], gate))
        elif kind == "T":
            here = after(seen[f"A{back}"], gate)
            made[name] = gate = term(padded, n, back * inner, True, local, here, seen[f"S{back}"])
        elif kind == "r":
            coming[f"R{back}"] = along(after(made[f"T{back}"], gate), -back)
    arrived = [coming["S0"]] + [coming[f"R{back}"] for back in range(1, outer)]
    return total(own, arrived)


def solution(mesh):
    in_specs = (
        P(("member", "col"), None, None),
        P(("member", "col"), None, None),
        P(("member", "col"), None, None),
        P(),
        P(("member", "col"), None),
        P(),
        P(),
    )
    out_specs = P(("member", "col"), None, None)
    run = functools.partial(body, mesh.shape["col"])
    return jax.shard_map(run, mesh=mesh, in_specs=in_specs, out_specs=out_specs, check_vma=False)
```

```python
import functools

import jax
import jax.numpy as jnp
from jax import lax
from jax.experimental import pallas as pl
from jax.experimental.pallas import tpu as pltpu
from jax.sharding import PartitionSpec as P

TOP = 32000.0
LANES = 16
UNROLL = 6


def pack(x, rows):
    largest = jnp.maximum(jnp.max(jnp.abs(x), axis=0, keepdims=True), 1e-30)
    power = jnp.ceil(jnp.log2(largest))
    part = jnp.ceil(largest * jnp.exp2(14.0 - power))
    value = jnp.round(x * (TOP / (part * jnp.exp2(power - 14.0))))
    row = lax.broadcasted_iota(jnp.int32, x.shape, 0)
    value = jnp.where(row == rows, power, jnp.where(row == rows + 1, part, value))
    return value.astype(jnp.int32).astype(jnp.int16)


def unpack(coded, rows):
    value = coded.astype(jnp.int32).astype(jnp.float32)
    scale = value[rows + 1 : rows + 2] * jnp.exp2(value[rows : rows + 1] - 14.0) * (1.0 / TOP)
    return value * scale


def term_kernel(n, which, count, packed, table, inc, jac, inn, cnt, iv, *refs):
    out, acc = refs[-2:]
    blocks, rows = inc.shape[:2]
    first, last = table[which], table[n + which]
    for l in range(blocks):
        acc[l] = jnp.zeros(acc.shape[1:], jnp.float32)
        if count:
            acc[l, :rows] = sum(unpack(coded[l], rows)[:rows] for coded in refs[:count])
    variance = iv[:, :1]

    def step(i, carry):
        terms = []
        for u in range(UNROLL):
            p = first + i * UNROLL + u
            entry = table[2 * n + jnp.minimum(p, last - 1)]
            b, l = entry // blocks, lax.rem(entry, blocks)
            live = (p < last).astype(jnp.float32)
            evolved = lax.dot_general(
                jac[b], inc[l], (((0,), (0,)), ((), ())), preferred_element_type=jnp.float32
            )
            weight = variance * (cnt[pl.ds(b, 1), :].astype(jnp.float32) * live)
            weighted = (weight * (evolved - inn[b].astype(jnp.float32))).astype(jnp.bfloat16)
            terms.append((l, jnp.dot(jac[b], weighted, preferred_element_type=jnp.float32)))
        for l, t in terms:
            acc[l, :rows] += t
        return carry

    lax.fori_loop(0, (last - first + UNROLL - 1) // UNROLL, step, 0)
    for l in range(blocks):
        out[l] = pack(acc[l], rows) if packed else acc[l, :rows]


def term(padded, n, which, packed, local, inc, *coded):
    table, jac, inn, cnt, iv = local
    smem = pl.BlockSpec(memory_space=pltpu.SMEM)
    vmem = pl.BlockSpec(memory_space=pltpu.VMEM)
    operands = [table, inc, jac, inn, cnt, iv, *coded]

    def shape(dtype, rows):
        return jax.ShapeDtypeStruct((inc.shape[0], rows, inc.shape[2]), dtype)

    return pl.pallas_call(
        functools.partial(term_kernel, n, which, len(coded), packed),
        out_shape=shape(jnp.int16, padded) if packed else shape(jnp.float32, inc.shape[1]),
        in_specs=[smem] + [vmem] * (len(operands) - 1),
        out_specs=vmem,
        scratch_shapes=[pltpu.VMEM((inc.shape[0], padded, inc.shape[2]), jnp.float32)],
        compiler_params=pltpu.CompilerParams(vmem_limit_bytes=16 * 2**20),
        cost_estimate=pl.CostEstimate(flops=2**20, bytes_accessed=8 * 2**20, transcendentals=0),
    )(*operands)


def order(outer):
    end = outer - 1
    if outer < 4:
        todo = [(kind, k) for k in range(1, outer) for kind in "zAy"]
        todo += [(kind, 0) for kind in "OBPs"]
        todo += [(kind, k) for k in range(1, outer) for kind in "BPs"]
        return todo + [(kind, k) for k in range(1, outer) for kind in "STr"]
    todo = [("z", end), ("A", 1), ("O", 0), ("z", 2), ("y", 1), ("B", 0), ("w", end), ("P", 0)]
    for k in range(2, end):
        todo += [("A", k), ("z", k + 1), ("y", k)] if k + 1 < end else [("A", k), ("y", k)]
        todo += [(kind, k - 1) for kind in "BPs"]
        if k > 3:
            todo += [(kind, k - 3) for kind in "STr"]
    todo += [(kind, end - 1) for kind in "BPs"]
    todo += [(kind, end) for kind in "ABPs"]
    todo += [(kind, k) for k in range(max(end - 3, 1), end) for kind in "STr"]
    return todo + [("s", 0), ("S", end), ("T", end), ("r", end)]


def at_hand_kernel(jac, inn, iv, turned, copied, column, whole, row, jac_sem, inn_sem, row_sem):
    count = jac_sem.shape[0]
    some = jac.shape[1] // count
    copy = pltpu.make_async_copy(inn, copied, inn_sem)
    parts = [
        pltpu.make_async_copy(jac.at[:, pl.ds(i * some, some)], whole.at[:, pl.ds(i * some, some)], jac_sem.at[i])
        for i in range(count)
    ]
    for part in parts:
        part.start()
    lead = pltpu.make_async_copy(iv, row, row_sem)
    lead.start()
    copy.start()
    for i, part in enumerate(parts):
        part.wait()
        turned[pl.ds(i * some, some)] = jnp.swapaxes(whole[:, pl.ds(i * some, some)], 0, 1)
    lead.wait()
    column[...] = jnp.swapaxes(jnp.broadcast_to(row[...], column.shape[::-1]), 0, 1)
    copy.wait()


def at_hand(jacobian, innovation, inv_variance):
    obs, channels, levels = jacobian.shape
    some = LANES if obs % LANES == 0 else obs
    hbm, vmem = pl.BlockSpec(memory_space=pltpu.HBM), pl.BlockSpec(memory_space=pltpu.VMEM)
    return pl.pallas_call(
        at_hand_kernel,
        out_shape=(
            pltpu.VMEM((obs, levels, channels), jacobian.dtype),
            pltpu.VMEM(innovation.shape, innovation.dtype),
            pltpu.VMEM((channels, 8), inv_variance.dtype),
        ),
        in_specs=[hbm, hbm, hbm],
        out_specs=(vmem, vmem, vmem),
        scratch_shapes=[
            pltpu.VMEM((levels, obs, channels), jacobian.dtype),
            pltpu.VMEM((1, channels), inv_variance.dtype),
            pltpu.SemaphoreType.DMA((obs // some,)),
            pltpu.SemaphoreType.DMA(()),
            pltpu.SemaphoreType.DMA(()),
        ],
        compiler_params=pltpu.CompilerParams(vmem_limit_bytes=24 * 2**20),
        cost_estimate=pl.CostEstimate(flops=2**20, bytes_accessed=10 * 2**20, transcendentals=0),
    )(
        pltpu.with_memory_space_constraint(jnp.transpose(jacobian, (2, 0, 1)), pltpu.HBM),
        pltpu.with_memory_space_constraint(innovation, pltpu.HBM),
        pltpu.with_memory_space_constraint(inv_variance[None, :], pltpu.HBM),
    )


def total_kernel(own, *refs):
    out = refs[-1]
    rows = own.shape[1]
    for l in range(own.shape[0]):
        total = own[l]
        for coded in refs[:-1]:
            total = total + unpack(coded[l], rows)[:rows]
        out[:, l, :] = total


def total(own, coded):
    vmem = pl.BlockSpec(memory_space=pltpu.VMEM)
    blocks, rows, columns = own.shape
    levels_first = pl.pallas_call(
        total_kernel,
        out_shape=jax.ShapeDtypeStruct((rows, blocks, columns), own.dtype),
        in_specs=[vmem] * (1 + len(coded)),
        out_specs=vmem,
        compiler_params=pltpu.CompilerParams(vmem_limit_bytes=16 * 2**20),
        cost_estimate=pl.CostEstimate(flops=2**20, bytes_accessed=8 * 2**20, transcendentals=0),
    )(own, *coded)
    return jnp.transpose(levels_first, (1, 0, 2))


def folded(count):
    return list(range(0, 1)) + list(range(1, count, 2)) + list(range((count - 1) // 2 * 2, 0, -2))


def after(x, gate):
    return x if isinstance(gate, tuple) and not gate else lax.optimization_barrier((x, gate))[0]


def sorted_table(owner, local_block, me, holders, obs, blocks):
    rows = lax.dynamic_slice_in_dim(owner[:, 0], me * obs, obs)
    local = lax.dynamic_slice_in_dim(local_block, me * obs, obs)
    index = jnp.arange(obs, dtype=jnp.int32)
    key = (rows * blocks + local) * obs + index
    place = jnp.sum(key[None, :] < key[:, None], axis=1, dtype=jnp.int32)
    entry = index * blocks + local
    order = jnp.sum(jnp.where(place[None, :] == index[:, None], entry[None, :], 0), axis=1, dtype=jnp.int32)
    first = jnp.sum(rows[None, :] < holders[:, None], axis=1, dtype=jnp.int32)
    last = jnp.sum(rows[None, :] <= holders[:, None], axis=1, dtype=jnp.int32)
    return jnp.concatenate([first, last, order])


def body(n, increment, jacobian, innovation, inv_variance, counts, owner, local_block):
    obs, channels, rows = jacobian.shape
    blocks = increment.shape[0]
    inner = 2
    outer = n // inner
    padded = -(-(rows + 2) // LANES) * LANES
    me = lax.axis_index("col")

    ring = folded(outer)

    def along(x, shift):
        lines = [(ring[p], ring[(p + shift) % outer]) for p in range(outer)]
        return lax.ppermute(x, "col", [(a * inner + r, b * inner + r) for a, b in lines for r in range(inner)])

    def across(x):
        return lax.ppermute(x, "col", [(i, i // inner * inner + (i + 1) % inner) for i in range(n)])

    inc = increment
    which = jnp.arange(n, dtype=jnp.int32)
    line = me // inner
    seat = jnp.where(line % 2 == 1, (line + 1) // 2, (outer - line // 2) % outer)
    seat = (seat + outer - which // inner) % outer
    line = jnp.where(2 * seat <= outer, jnp.maximum(2 * seat - 1, 0), 2 * (outer - seat))
    holders = line * inner + (me + which) % inner
    table = sorted_table(owner, local_block, me, holders, obs, blocks)
    jac, inn, variance = at_hand(jacobian, innovation, inv_variance)
    local = (table, jac, inn, counts, variance)

    coming = {"B0": across(inc)}
    if outer > 1:
        coming["A1"] = along(inc, 1)
    seen, made, gate = {"A0": inc}, {}, ()
    for kind, back in order(outer):
        name = f"{kind}{back}"
        if kind in "ABS":
            seen[name] = gate = after(coming[name], gate)
        elif kind == "z":
            source, shift = (seen[f"A{back - 1}"], 1) if back < outer - 1 else (inc, -1)
            coming[f"A{back}"] = along(after(source, gate), shift)
        elif kind == "y":
            coming[f"B{back}"] = across(after(seen[f"A{back}"], gate))
        elif kind == "w":
            coming[f"B{back}"] = along(after(seen["B0"], gate), -1)
        elif kind == "O":
            own = gate = term(padded, n, 0, False, local, inc)
        elif kind == "P":
            made[name] = gate = term(padded, n, back * inner + 1, True, local, after(seen[f"B{back}"], gate))
        elif kind == "s":
            coming[f"S{back}"] = across(after(made[f"P{back}"], gate))
        elif kind == "T":
            here = after(seen[f"A{back}"], gate)
            made[name] = gate = term(padded, n, back * inner, True, local, here, seen[f"S{back}"])
        elif kind == "r":
            coming[f"R{back}"] = along(after(made[f"T{back}"], gate), -back)
    arrived = [coming["S0"]] + [coming[f"R{back}"] for back in range(1, outer)]
    return total(own, arrived)


def solution(mesh):
    in_specs = (
        P(("member", "col"), None, None),
        P(("member", "col"), None, None),
        P(("member", "col"), None, None),
        P(),
        P(("member", "col"), None),
        P(),
        P(),
    )
    out_specs = P(("member", "col"), None, None)
    run = functools.partial(body, mesh.shape["col"])
    return jax.shard_map(run, mesh=mesh, in_specs=in_specs, out_specs=out_specs, check_vma=False)
```

```python
import functools

import jax
import jax.numpy as jnp
from jax import lax
from jax.experimental import pallas as pl
from jax.experimental.pallas import tpu as pltpu
from jax.sharding import PartitionSpec as P

TOP = 32000.0
LANES = 16
UNROLL = 6


def pack(x, rows):
    largest = jnp.maximum(jnp.max(jnp.abs(x), axis=0, keepdims=True), 1e-30)
    power = jnp.ceil(jnp.log2(largest))
    part = jnp.ceil(largest * jnp.exp2(14.0 - power))
    value = jnp.round(x * (TOP / (part * jnp.exp2(power - 14.0))))
    row = lax.broadcasted_iota(jnp.int32, x.shape, 0)
    value = jnp.where(row == rows, power, jnp.where(row == rows + 1, part, value))
    return value.astype(jnp.int32).astype(jnp.int16)


def unpack(coded, rows):
    value = coded.astype(jnp.int32).astype(jnp.float32)
    scale = value[rows + 1 : rows + 2] * jnp.exp2(value[rows : rows + 1] - 14.0) * (1.0 / TOP)
    return value * scale


def term_kernel(n, which, count, packed, table, inc, jac, inn, cnt, iv, *refs):
    out, acc = refs[-2:]
    blocks, rows = inc.shape[:2]
    first, last = table[which], table[n + which]
    for l in range(blocks):
        acc[l] = jnp.zeros(acc.shape[1:], jnp.float32)
        if count:
            acc[l, :rows] = sum(unpack(coded[l], rows)[:rows] for coded in refs[:count])
    variance = iv[:, :1]

    def step(i, carry):
        terms = []
        for u in range(UNROLL):
            p = first + i * UNROLL + u
            entry = table[2 * n + jnp.minimum(p, last - 1)]
            b, l = entry // blocks, lax.rem(entry, blocks)
            live = (p < last).astype(jnp.float32)
            evolved = lax.dot_general(
                jac[b], inc[l], (((0,), (0,)), ((), ())), preferred_element_type=jnp.float32
            )
            weight = variance * (cnt[pl.ds(b, 1), :].astype(jnp.float32) * live)
            weighted = (weight * (evolved - inn[b].astype(jnp.float32))).astype(jnp.bfloat16)
            terms.append((l, jnp.dot(jac[b], weighted, preferred_element_type=jnp.float32)))
        for l, t in terms:
            acc[l, :rows] += t
        return carry

    lax.fori_loop(0, (last - first + UNROLL - 1) // UNROLL, step, 0)
    for l in range(blocks):
        out[l] = pack(acc[l], rows) if packed else acc[l, :rows]


def term(padded, n, which, packed, local, inc, *coded):
    table, jac, inn, cnt, iv = local
    smem = pl.BlockSpec(memory_space=pltpu.SMEM)
    vmem = pl.BlockSpec(memory_space=pltpu.VMEM)
    operands = [table, inc, jac, inn, cnt, iv, *coded]

    def shape(dtype, rows):
        return jax.ShapeDtypeStruct((inc.shape[0], rows, inc.shape[2]), dtype)

    return pl.pallas_call(
        functools.partial(term_kernel, n, which, len(coded), packed),
        out_shape=shape(jnp.int16, padded) if packed else shape(jnp.float32, inc.shape[1]),
        in_specs=[smem] + [vmem] * (len(operands) - 1),
        out_specs=vmem,
        scratch_shapes=[pltpu.VMEM((inc.shape[0], padded, inc.shape[2]), jnp.float32)],
        compiler_params=pltpu.CompilerParams(vmem_limit_bytes=16 * 2**20),
        cost_estimate=pl.CostEstimate(flops=2**20, bytes_accessed=8 * 2**20, transcendentals=0),
    )(*operands)


def order(outer):
    end = outer - 1
    if outer < 4:
        todo = [(kind, k) for k in range(1, outer) for kind in "zAy"]
        todo += [(kind, 0) for kind in "OBPs"]
        todo += [(kind, k) for k in range(1, outer) for kind in "BPs"]
        return todo + [(kind, k) for k in range(1, outer) for kind in "STr"]
    todo = [("z", end), ("L", 0), ("A", 1), ("z", 2), ("y", 1), ("B", 0), ("P", 0)]
    for k in range(2, end):
        todo += [("A", k), ("z", k + 1), ("y", k)] if k + 1 < end else [("A", k), ("y", k)]
        todo += [("B", k - 1), ("P", k - 1)] + [("w", end)] * (k == 2) + [("s", k - 1)] + [("O", 0)] * (k == 2)
        if k > 3:
            todo += [(kind, k - 3) for kind in "STr"]
    todo += [(kind, end - 1) for kind in "BPs"]
    todo += [(kind, end) for kind in "ABPs"]
    todo += [(kind, k) for k in range(max(end - 3, 1), end) for kind in "STr"]
    return todo + [("s", 0), ("S", end), ("T", end), ("r", end)]


def at_hand_kernel(jac, inn, iv, turned, copied, column, whole, row, jac_sem, inn_sem, row_sem):
    count = jac_sem.shape[0]
    some = jac.shape[1] // count
    copy = pltpu.make_async_copy(inn, copied, inn_sem)
    parts = [
        pltpu.make_async_copy(jac.at[:, pl.ds(i * some, some)], whole.at[:, pl.ds(i * some, some)], jac_sem.at[i])
        for i in range(count)
    ]
    for part in parts:
        part.start()
    lead = pltpu.make_async_copy(iv, row, row_sem)
    lead.start()
    copy.start()
    for i, part in enumerate(parts):
        part.wait()
        turned[pl.ds(i * some, some)] = jnp.swapaxes(whole[:, pl.ds(i * some, some)], 0, 1)
    lead.wait()
    column[...] = jnp.swapaxes(jnp.broadcast_to(row[...], column.shape[::-1]), 0, 1)
    copy.wait()


def at_hand(jacobian, innovation, inv_variance):
    obs, channels, levels = jacobian.shape
    some = LANES if obs % LANES == 0 else obs
    hbm, vmem = pl.BlockSpec(memory_space=pltpu.HBM), pl.BlockSpec(memory_space=pltpu.VMEM)
    return pl.pallas_call(
        at_hand_kernel,
        out_shape=(
            pltpu.VMEM((obs, levels, channels), jacobian.dtype),
            pltpu.VMEM(innovation.shape, innovation.dtype),
            pltpu.VMEM((channels, 8), inv_variance.dtype),
        ),
        in_specs=[hbm, hbm, hbm],
        out_specs=(vmem, vmem, vmem),
        scratch_shapes=[
            pltpu.VMEM((levels, obs, channels), jacobian.dtype),
            pltpu.VMEM((1, channels), inv_variance.dtype),
            pltpu.SemaphoreType.DMA((obs // some,)),
            pltpu.SemaphoreType.DMA(()),
            pltpu.SemaphoreType.DMA(()),
        ],
        compiler_params=pltpu.CompilerParams(vmem_limit_bytes=24 * 2**20),
        cost_estimate=pl.CostEstimate(flops=2**20, bytes_accessed=10 * 2**20, transcendentals=0),
    )(
        pltpu.with_memory_space_constraint(jnp.transpose(jacobian, (2, 0, 1)), pltpu.HBM),
        pltpu.with_memory_space_constraint(innovation, pltpu.HBM),
        pltpu.with_memory_space_constraint(inv_variance[None, :], pltpu.HBM),
    )


def total_kernel(own, *refs):
    out = refs[-1]
    rows = own.shape[1]
    for l in range(own.shape[0]):
        total = own[l]
        for coded in refs[:-1]:
            total = total + unpack(coded[l], rows)[:rows]
        out[:, l, :] = total


def total(own, coded):
    vmem = pl.BlockSpec(memory_space=pltpu.VMEM)
    blocks, rows, columns = own.shape
    levels_first = pl.pallas_call(
        total_kernel,
        out_shape=jax.ShapeDtypeStruct((rows, blocks, columns), own.dtype),
        in_specs=[vmem] * (1 + len(coded)),
        out_specs=vmem,
        compiler_params=pltpu.CompilerParams(vmem_limit_bytes=16 * 2**20),
        cost_estimate=pl.CostEstimate(flops=2**20, bytes_accessed=8 * 2**20, transcendentals=0),
    )(own, *coded)
    return jnp.transpose(levels_first, (1, 0, 2))


def folded(count):
    return list(range(0, 1)) + list(range(1, count, 2)) + list(range((count - 1) // 2 * 2, 0, -2))


def after(x, gate):
    return x if isinstance(gate, tuple) and not gate else lax.optimization_barrier((x, gate))[0]


def sorted_table(owner, local_block, me, holders, obs, blocks):
    rows = lax.dynamic_slice_in_dim(owner[:, 0], me * obs, obs)
    local = lax.dynamic_slice_in_dim(local_block, me * obs, obs)
    index = jnp.arange(obs, dtype=jnp.int32)
    key = (rows * blocks + local) * obs + index
    place = jnp.sum(key[None, :] < key[:, None], axis=1, dtype=jnp.int32)
    entry = index * blocks + local
    order = jnp.sum(jnp.where(place[None, :] == index[:, None], entry[None, :], 0), axis=1, dtype=jnp.int32)
    first = jnp.sum(rows[None, :] < holders[:, None], axis=1, dtype=jnp.int32)
    last = jnp.sum(rows[None, :] <= holders[:, None], axis=1, dtype=jnp.int32)
    return jnp.concatenate([first, last, order])


def body(n, increment, jacobian, innovation, inv_variance, counts, owner, local_block):
    obs, channels, rows = jacobian.shape
    blocks = increment.shape[0]
    inner = 2
    outer = n // inner
    padded = -(-(rows + 2) // LANES) * LANES
    me = lax.axis_index("col")

    ring = folded(outer)

    def along(x, shift):
        lines = [(ring[p], ring[(p + shift) % outer]) for p in range(outer)]
        return lax.ppermute(x, "col", [(a * inner + r, b * inner + r) for a, b in lines for r in range(inner)])

    def across(x):
        return lax.ppermute(x, "col", [(i, i // inner * inner + (i + 1) % inner) for i in range(n)])

    inc = increment
    which = jnp.arange(n, dtype=jnp.int32)
    line = me // inner
    seat = jnp.where(line % 2 == 1, (line + 1) // 2, (outer - line // 2) % outer)
    seat = (seat + outer - which // inner) % outer
    line = jnp.where(2 * seat <= outer, jnp.maximum(2 * seat - 1, 0), 2 * (outer - seat))
    holders = line * inner + (me + which) % inner
    table = sorted_table(owner, local_block, me, holders, obs, blocks)
    jac, inn, variance = at_hand(jacobian, innovation, inv_variance)
    local = (table, jac, inn, counts, variance)

    coming = {"B0": across(inc)}
    if outer > 1:
        coming["A1"] = along(inc, 1)
    seen, made, gate = {"A0": inc}, {}, ()
    for kind, back in order(outer):
        name = f"{kind}{back}"
        if kind in "ABS":
            seen[name] = gate = after(coming[name], gate)
        elif kind == "z":
            source, shift = (seen[f"A{back - 1}"], 1) if back < outer - 1 else (inc, -1)
            coming[f"A{back}"] = along(after(source, gate), shift)
        elif kind == "y":
            coming[f"B{back}"] = across(after(seen[f"A{back}"], gate))
        elif kind == "w":
            coming[f"B{back}"] = along(after(seen["B0"], gate), -1)
        elif kind == "L":
            gate = (jac, inn)
        elif kind == "O":
            own = gate = term(padded, n, 0, False, local, inc)
        elif kind == "P":
            made[name] = gate = term(padded, n, back * inner + 1, True, local, after(seen[f"B{back}"], gate))
        elif kind == "s":
            coming[f"S{back}"] = across(after(made[f"P{back}"], gate))
        elif kind == "T":
            here = after(seen[f"A{back}"], gate)
            made[name] = gate = term(padded, n, back * inner, True, local, here, seen[f"S{back}"])
        elif kind == "r":
            coming[f"R{back}"] = along(after(made[f"T{back}"], gate), -back)
    arrived = [coming[name] for name in coming if name[0] == "R" or name == "S0"]
    return total(own, arrived)


def solution(mesh):
    in_specs = (
        P(("member", "col"), None, None),
        P(("member", "col"), None, None),
        P(("member", "col"), None, None),
        P(),
        P(("member", "col"), None),
        P(),
        P(),
    )
    out_specs = P(("member", "col"), None, None)
    run = functools.partial(body, mesh.shape["col"])
    return jax.shard_map(run, mesh=mesh, in_specs=in_specs, out_specs=out_specs, check_vma=False)
```

```python
import functools

import jax
import jax.numpy as jnp
from jax import lax
from jax.experimental import pallas as pl
from jax.experimental.pallas import tpu as pltpu
from jax.sharding import PartitionSpec as P

TOP = 32000.0
LANES = 16
UNROLL = 6


def pack(x, rows):
    largest = jnp.maximum(jnp.max(jnp.abs(x), axis=0, keepdims=True), 1e-30)
    power = jnp.ceil(jnp.log2(largest))
    part = jnp.ceil(largest * jnp.exp2(14.0 - power))
    value = jnp.round(x * (TOP / (part * jnp.exp2(power - 14.0))))
    row = lax.broadcasted_iota(jnp.int32, x.shape, 0)
    value = jnp.where(row == rows, power, jnp.where(row == rows + 1, part, value))
    return value.astype(jnp.int32).astype(jnp.int16)


def unpack(coded, rows):
    value = coded.astype(jnp.int32).astype(jnp.float32)
    scale = value[rows + 1 : rows + 2] * jnp.exp2(value[rows : rows + 1] - 14.0) * (1.0 / TOP)
    return value * scale


def term_kernel(n, which, count, packed, table, inc, jac, inn, cnt, iv, *refs):
    out, acc = refs[-2:]
    blocks, rows = inc.shape[:2]
    first, last = table[which], table[n + which]
    for l in range(blocks):
        acc[l] = jnp.zeros(acc.shape[1:], jnp.float32)
        if count:
            acc[l, :rows] = sum(unpack(coded[l], rows)[:rows] for coded in refs[:count])
    variance = iv[:, :1]

    def step(i, carry):
        terms = []
        for u in range(UNROLL):
            p = first + i * UNROLL + u
            entry = table[2 * n + jnp.minimum(p, last - 1)]
            b, l = entry // blocks, lax.rem(entry, blocks)
            live = (p < last).astype(jnp.float32)
            evolved = lax.dot_general(
                jac[b], inc[l], (((0,), (0,)), ((), ())), preferred_element_type=jnp.float32
            )
            weight = variance * (cnt[pl.ds(b, 1), :].astype(jnp.float32) * live)
            weighted = (weight * (evolved - inn[b].astype(jnp.float32))).astype(jnp.bfloat16)
            terms.append((l, jnp.dot(jac[b], weighted, preferred_element_type=jnp.float32)))
        for l, t in terms:
            acc[l, :rows] += t
        return carry

    lax.fori_loop(0, (last - first + UNROLL - 1) // UNROLL, step, 0)
    for l in range(blocks):
        out[l] = pack(acc[l], rows) if packed else acc[l, :rows]


def term(padded, n, which, packed, local, inc, *coded):
    table, jac, inn, cnt, iv = local
    smem = pl.BlockSpec(memory_space=pltpu.SMEM)
    vmem = pl.BlockSpec(memory_space=pltpu.VMEM)
    operands = [table, inc, jac, inn, cnt, iv, *coded]

    def shape(dtype, rows):
        return jax.ShapeDtypeStruct((inc.shape[0], rows, inc.shape[2]), dtype)

    return pl.pallas_call(
        functools.partial(term_kernel, n, which, len(coded), packed),
        out_shape=shape(jnp.int16, padded) if packed else shape(jnp.float32, inc.shape[1]),
        in_specs=[smem] + [vmem] * (len(operands) - 1),
        out_specs=vmem,
        scratch_shapes=[pltpu.VMEM((inc.shape[0], padded, inc.shape[2]), jnp.float32)],
        compiler_params=pltpu.CompilerParams(vmem_limit_bytes=16 * 2**20),
        cost_estimate=pl.CostEstimate(flops=2**20, bytes_accessed=8 * 2**20, transcendentals=0),
    )(*operands)


def order(outer):
    end = outer - 1
    if outer < 4:
        todo = [(kind, k) for k in range(1, outer) for kind in "zAy"]
        todo += [(kind, 0) for kind in "OBPs"]
        todo += [(kind, k) for k in range(1, outer) for kind in "BPs"]
        return todo + [(kind, k) for k in range(1, outer) for kind in "STr"]
    todo = [("z", end), ("L", 0), ("A", 1), ("z", 2), ("y", 1), ("O", 0), ("B", 0)]
    for k in range(2, end):
        todo += [("A", k), ("z", k + 1), ("y", k)] if k + 1 < end else [("A", k), ("y", k)]
        todo += [("B", k - 1), ("P", k - 1)] + [("w", end)] * (k == 2) + [("s", k - 1)] + [("P", 0)] * (k == 2)
        if k > 3:
            todo += [(kind, k - 3) for kind in "STr"]
    todo += [(kind, end - 1) for kind in "BPs"]
    todo += [(kind, end) for kind in "ABPs"]
    todo += [(kind, k) for k in range(max(end - 3, 1), end) for kind in "STr"]
    return todo + [("s", 0), ("S", end), ("T", end), ("r", end)]


def at_hand_kernel(jac, inn, iv, turned, copied, column, whole, row, jac_sem, inn_sem, row_sem):
    count = jac_sem.shape[0]
    some = jac.shape[1] // count
    copy = pltpu.make_async_copy(inn, copied, inn_sem)
    parts = [
        pltpu.make_async_copy(jac.at[:, pl.ds(i * some, some)], whole.at[:, pl.ds(i * some, some)], jac_sem.at[i])
        for i in range(count)
    ]
    for part in parts:
        part.start()
    lead = pltpu.make_async_copy(iv, row, row_sem)
    lead.start()
    copy.start()
    for i, part in enumerate(parts):
        part.wait()
        turned[pl.ds(i * some, some)] = jnp.swapaxes(whole[:, pl.ds(i * some, some)], 0, 1)
    lead.wait()
    column[...] = jnp.swapaxes(jnp.broadcast_to(row[...], column.shape[::-1]), 0, 1)
    copy.wait()


def at_hand(jacobian, innovation, inv_variance):
    obs, channels, levels = jacobian.shape
    some = LANES if obs % LANES == 0 else obs
    hbm, vmem = pl.BlockSpec(memory_space=pltpu.HBM), pl.BlockSpec(memory_space=pltpu.VMEM)
    return pl.pallas_call(
        at_hand_kernel,
        out_shape=(
            pltpu.VMEM((obs, levels, channels), jacobian.dtype),
            pltpu.VMEM(innovation.shape, innovation.dtype),
            pltpu.VMEM((channels, 8), inv_variance.dtype),
        ),
        in_specs=[hbm, hbm, hbm],
        out_specs=(vmem, vmem, vmem),
        scratch_shapes=[
            pltpu.VMEM((levels, obs, channels), jacobian.dtype),
            pltpu.VMEM((1, channels), inv_variance.dtype),
            pltpu.SemaphoreType.DMA((obs // some,)),
            pltpu.SemaphoreType.DMA(()),
            pltpu.SemaphoreType.DMA(()),
        ],
        compiler_params=pltpu.CompilerParams(vmem_limit_bytes=24 * 2**20),
        cost_estimate=pl.CostEstimate(flops=2**20, bytes_accessed=10 * 2**20, transcendentals=0),
    )(
        pltpu.with_memory_space_constraint(jnp.transpose(jacobian, (2, 0, 1)), pltpu.HBM),
        pltpu.with_memory_space_constraint(innovation, pltpu.HBM),
        pltpu.with_memory_space_constraint(inv_variance[None, :], pltpu.HBM),
    )


def total_kernel(own, *refs):
    out = refs[-1]
    rows = own.shape[1]
    for l in range(own.shape[0]):
        total = own[l]
        for coded in refs[:-1]:
            total = total + unpack(coded[l], rows)[:rows]
        out[:, l, :] = total


def total(own, coded):
    vmem = pl.BlockSpec(memory_space=pltpu.VMEM)
    blocks, rows, columns = own.shape
    levels_first = pl.pallas_call(
        total_kernel,
        out_shape=jax.ShapeDtypeStruct((rows, blocks, columns), own.dtype),
        in_specs=[vmem] * (1 + len(coded)),
        out_specs=vmem,
        compiler_params=pltpu.CompilerParams(vmem_limit_bytes=16 * 2**20),
        cost_estimate=pl.CostEstimate(flops=2**20, bytes_accessed=8 * 2**20, transcendentals=0),
    )(own, *coded)
    return jnp.transpose(levels_first, (1, 0, 2))


def folded(count):
    return list(range(0, 1)) + list(range(1, count, 2)) + list(range((count - 1) // 2 * 2, 0, -2))


def after(x, gate):
    return x if isinstance(gate, tuple) and not gate else lax.optimization_barrier((x, gate))[0]


def sorted_table(owner, local_block, me, holders, obs, blocks):
    rows = lax.dynamic_slice_in_dim(owner[:, 0], me * obs, obs)
    local = lax.dynamic_slice_in_dim(local_block, me * obs, obs)
    index = jnp.arange(obs, dtype=jnp.int32)
    key = (rows * blocks + local) * obs + index
    place = jnp.sum(key[None, :] < key[:, None], axis=1, dtype=jnp.int32)
    entry = index * blocks + local
    order = jnp.sum(jnp.where(place[None, :] == index[:, None], entry[None, :], 0), axis=1, dtype=jnp.int32)
    first = jnp.sum(rows[None, :] < holders[:, None], axis=1, dtype=jnp.int32)
    last = jnp.sum(rows[None, :] <= holders[:, None], axis=1, dtype=jnp.int32)
    return jnp.concatenate([first, last, order])


def body(n, increment, jacobian, innovation, inv_variance, counts, owner, local_block):
    obs, channels, rows = jacobian.shape
    blocks = increment.shape[0]
    inner = 2
    outer = n // inner
    padded = -(-(rows + 2) // LANES) * LANES
    me = lax.axis_index("col")

    ring = folded(outer)

    def along(x, shift):
        lines = [(ring[p], ring[(p + shift) % outer]) for p in range(outer)]
        return lax.ppermute(x, "col", [(a * inner + r, b * inner + r) for a, b in lines for r in range(inner)])

    def across(x):
        return lax.ppermute(x, "col", [(i, i // inner * inner + (i + 1) % inner) for i in range(n)])

    inc = increment
    which = jnp.arange(n, dtype=jnp.int32)
    line = me // inner
    seat = jnp.where(line % 2 == 1, (line + 1) // 2, (outer - line // 2) % outer)
    seat = (seat + outer - which // inner) % outer
    line = jnp.where(2 * seat <= outer, jnp.maximum(2 * seat - 1, 0), 2 * (outer - seat))
    holders = line * inner + (me + which) % inner
    table = sorted_table(owner, local_block, me, holders, obs, blocks)
    jac, inn, variance = at_hand(jacobian, innovation, inv_variance)
    local = (table, jac, inn, counts, variance)

    coming = {"B0": across(inc)}
    if outer > 1:
        coming["A1"] = along(inc, 1)
    seen, made, gate = {"A0": inc}, {}, ()
    for kind, back in order(outer):
        name = f"{kind}{back}"
        if kind in "ABS":
            seen[name] = gate = after(coming[name], gate)
        elif kind == "z":
            source, shift = (seen[f"A{back - 1}"], 1) if back < outer - 1 else (inc, -1)
            coming[f"A{back}"] = along(after(source, gate), shift)
        elif kind == "y":
            coming[f"B{back}"] = across(after(seen[f"A{back}"], gate))
        elif kind == "w":
            coming[f"B{back}"] = along(after(seen["B0"], gate), -1)
        elif kind == "L":
            gate = (jac, inn)
        elif kind == "O":
            own = gate = term(padded, n, 0, False, local, inc)
        elif kind == "P":
            made[name] = gate = term(padded, n, back * inner + 1, True, local, after(seen[f"B{back}"], gate))
        elif kind == "s":
            coming[f"S{back}"] = across(after(made[f"P{back}"], gate))
        elif kind == "T":
            here = after(seen[f"A{back}"], gate)
            made[name] = gate = term(padded, n, back * inner, True, local, here, seen[f"S{back}"])
        elif kind == "r":
            coming[f"R{back}"] = along(after(made[f"T{back}"], gate), -back)
    arrived = [coming[name] for name in coming if name[0] == "R" or name == "S0"]
    return total(own, arrived)


def solution(mesh):
    in_specs = (
        P(("member", "col"), None, None),
        P(("member", "col"), None, None),
        P(("member", "col"), None, None),
        P(),
        P(("member", "col"), None),
        P(),
        P(),
    )
    out_specs = P(("member", "col"), None, None)
    run = functools.partial(body, mesh.shape["col"])
    return jax.shard_map(run, mesh=mesh, in_specs=in_specs, out_specs=out_specs, check_vma=False)
```
